32 devices in a mesh: groups: 2 (over x), dp: 8 (over z, y), tensor: 2 (over core).
Axes of the slice: x: 2, y: 2, z: 4, core: 2. Of those that a mesh axis runs over, the one named last changes fastest.
Arguments:
- x_in: bfloat16 [1536, 8192], P(('groups', 'dp'), 'tensor'), parts along dimension 0, may hold values from -6 to 6
- gate_pre: bfloat16 [1536, 28672], P(('groups', 'dp'), 'tensor'), parts along dimension 0, may hold values from -6 to 6
- up_pre: bfloat16 [1536, 28672], P(('groups', 'dp'), 'tensor'), parts along dimension 0, may hold values from -6 to 6
- grad_hidden: bfloat16 [1536, 28672], P(('groups', 'dp'), 'tensor'), parts along dimension 0, may hold values from -6 to 6
- grad_out: bfloat16 [1536, 8192], P(('groups', 'dp'), 'tensor'), parts along dimension 0, may hold values from -6 to 6
- proj_model: bfloat16 [64, 8192], P('dp', 'tensor'), may hold values from -0.0625 to 0.0625
- proj_hidden: bfloat16 [64, 28672], P('dp', 'tensor'), may hold values from -0.03125 to 0.03125
- lengths: int32 [8], P('groups'), parts along dimension 0, may hold values from 1 to 384, 768 in all
- queries: bfloat16 [512, 12288], P(('groups', 'dp'), 'tensor'), parts along dimension 0, may hold values from -0.0546875 to 0.0546875
- cand: int32 [8, 8], P('groups'), parts along dimension 0, may hold values from 0 to 7
- cand_count: int32 [8], P('groups'), parts along dimension 0, may hold values from 1 to 8
Outputs:
- scores: float32 [8, 8, 32], P('groups'), parts along dimension 0
The draws below stay inside these ranges and needn't reach their ends.
There are 2 independent parts, one for each index of `groups`. The reference program is written for one: setup_inputs(seed, part) draws one part's arguments, and reference() takes and returns one part's arrays. A program takes and returns all parts, laid end to end along the dimension named above; an argument that names none is the same for every part. Nothing has to cross between parts.
Inputs may be any that keep to these rules, and one draw needn't show every extreme that they name: The lengths sum to 768; sequence s occupies the tokens that follow those of sequences 0 to s - 1.
All inputs are finite; a program needn't handle non-finite values.
Results may differ from the reference program's by a relative error of at most 0.0042.
Values may be sent and summed in bfloat16 or wider, within the bound.
A program may use at most 64 MiB of HBM per device.

```python
import math
import jax
import jax.numpy as jnp
import numpy as np
from jax import lax

D = 8192
FF = 28672
RANK = 64
TOK_DEV = 96
SEQS = 4
QBS = 32
CAND = 8
TOKENS = 768
MOST = 384
QB = 8
QUERIES = 256


def place_ends(values, key, least, high):
    longest = values.shape.index(max(values.shape))
    spots = []
    for shift in (0, 1):
        where = [jax.random.randint(jax.random.fold_in(key, axis), (), 0, length) for axis, length in enumerate(values.shape)]
        where[longest] = (where[longest] + shift) % values.shape[longest]
        spots.append(tuple(where))
    return values.at[spots[0]].set(least).at[spots[1]].set(high)


def level_of(stream_key, shape, pieces, smallest, top_value):
    factor_of, own = 1.0, jax.random.fold_in(stream_key, 6)
    for dim, blocks in pieces:
        draws = jnp.exp(jax.random.uniform(jax.random.fold_in(own, dim), (blocks,), jnp.float32, smallest / len(pieces), top_value / len(pieces)))
        factor_of = factor_of * jnp.repeat(draws, shape[dim] // blocks).reshape([-1 if axis == dim else 1 for axis in range(len(shape))])
    return factor_of


def split_up(amount, total, bound, skew):
    weights = [(1 << 20) // math.isqrt(standing ** skew) + 1 for standing in range(2, amount + 1)]
    surplus, holding = total - bound - (amount - 1), [1] * (amount - 1)
    while surplus > 0:
        movable = [i for i in range(amount - 1) if holding[i] < bound]
        mass, left = sum([weights[i] for i in movable]), surplus
        for i in movable:
            extra = min(bound - holding[i], max(1, left * weights[i] // mass), surplus)
            holding[i] = holding[i] + extra
            surplus = surplus - extra
    return np.array([bound] + holding)


def ragged_sizes(own_key, amount, total, bound, slope):
    if amount == 2:
        one = jax.random.randint(own_key, (), max(1, total - bound), min(bound, total - 1) + 1)
        return jnp.stack([one, total - one])
    sizes = jnp.asarray(split_up(amount, total, bound, slope), jnp.int32)
    twos = (amount - 1) // 2
    source_of, receiver = sizes[1:1 + 2 * twos:2], sizes[2:2 + 2 * twos:2]
    margin = jnp.minimum(source_of - 1, bound - receiver)
    passed = jax.random.randint(jax.random.fold_in(own_key, 1), (twos,), 0, 1 << 20) % (margin + 1)
    sizes = sizes.at[1:1 + 2 * twos:2].set(source_of - passed).at[2:2 + 2 * twos:2].set(receiver + passed)
    return sizes[jax.random.permutation(jax.random.fold_in(own_key, 2), amount)]


def centred(own_key, extent, spread, bound, shards=(), held_as=jnp.bfloat16):
    array = jax.random.normal(own_key, extent, jnp.float32) * spread
    if len(shards) > 0:
        array = level_of(own_key, extent, shards, -0.22, 0.18) * array
    return jnp.clip(array, min=-bound, max=bound).astype(held_as)


def setup_inputs(seed: int = 0, part: int = 0) -> dict:
    streams_of = jax.random.split(jax.random.key(seed), 12)
    part_keys = jax.random.split(jax.random.fold_in(streams_of[11], part), 12)
    x_in = centred(part_keys[0], (TOKENS, D), 1.0, 6.0, ((0, 8), (1, 2)))
    gate_pre = centred(part_keys[1], (TOKENS, FF), 1.0, 6.0, ((0, 8), (1, 2)))
    up_pre = centred(part_keys[2], (TOKENS, FF), 1.0, 6.0, ((0, 8), (1, 2)))
    grad_hidden = centred(part_keys[3], (TOKENS, FF), 1.0, 6.0, ((0, 8), (1, 2)))
    grad_out = centred(part_keys[4], (TOKENS, D), 1.0, 6.0, ((0, 8), (1, 2)))
    proj_model = centred(streams_of[5], (RANK, D), D ** -0.5, 0.0625, ((0, 8), (1, 2)))
    proj_hidden = centred(streams_of[6], (RANK, FF), FF ** -0.5, 0.03125, ((0, 8), (1, 2)))
    lengths = ragged_sizes(part_keys[7], SEQS, TOKENS, MOST, 2).astype(jnp.int32)
    queries = centred(part_keys[8], (QUERIES, 3 * RANK * RANK), (3 * RANK * RANK) ** -0.5, 0.0546875, ((0, 8), (1, 2)))
    cand = place_ends(jax.random.randint(part_keys[9], (SEQS, CAND), 0, QB), jax.random.fold_in(part_keys[9], 1), 0, QB - 1).astype(jnp.int32)
    cand_count = place_ends(jax.random.randint(part_keys[10], (SEQS,), 1, CAND + 1), jax.random.fold_in(part_keys[10], 1), 1, CAND).astype(jnp.int32)
    return dict(x_in=x_in, gate_pre=gate_pre, up_pre=up_pre, grad_hidden=grad_hidden, grad_out=grad_out, proj_model=proj_model, proj_hidden=proj_hidden, lengths=lengths, queries=queries, cand=cand, cand_count=cand_count)


def contract_rows(left, right):
    return lax.dot_general(left, right, (((1,), (1,)), ((), ())), preferred_element_type=jnp.float32)

def reference(x_in, gate_pre, up_pre, grad_hidden, grad_out, proj_model, proj_hidden, lengths, queries, cand, cand_count):

    def project(inputs):
        x_blk, gate_blk, up_blk, grad_blk, out_blk = inputs
        gate_f = gate_blk.astype(jnp.float32)
        up_f = up_blk.astype(jnp.float32)
        grad_f = grad_blk.astype(jnp.float32)
        sig_gate = jax.nn.sigmoid(gate_f)
        hidden_act = (gate_f * sig_gate * up_f).astype(jnp.bfloat16)
        grad_gate = (grad_f * up_f * sig_gate * (1.0 + gate_f * (1.0 - sig_gate))).astype(jnp.bfloat16)
        grad_up = (grad_f * gate_f * sig_gate).astype(jnp.bfloat16)
        return (contract_rows(x_blk, proj_model), contract_rows(hidden_act, proj_hidden), contract_rows(grad_gate, proj_hidden), contract_rows(grad_up, proj_hidden), contract_rows(out_blk, proj_model))
    blocks_n = TOKENS // TOK_DEV

    def split(arr):
        return arr.reshape(blocks_n, TOK_DEV, arr.shape[1])
    outs_all = lax.map(project, (split(x_in), split(gate_pre), split(up_pre), split(grad_hidden), split(grad_out)))
    model_proj, hidden_proj, gate_proj, up_proj, out_proj = [o.reshape(TOKENS, RANK) for o in outs_all]
    position = jnp.arange(TOKENS, dtype=jnp.int32)
    seq_ends = jnp.cumsum(lengths).astype(jnp.int32)
    seq_of = lax.optimization_barrier(jnp.sum((seq_ends[None, :] <= position[:, None]).astype(jnp.int32), axis=1))
    onehot = (seq_of[:, None] == jnp.arange(SEQS, dtype=jnp.int32)[None, :]).astype(jnp.float32)

    def gram_sum(out_vecs, in_vecs):
        left = (onehot[:, :, None] * out_vecs[:, None, :]).reshape(TOKENS, SEQS * RANK)
        return jnp.dot(left.T, in_vecs, precision=lax.Precision.HIGHEST).reshape(SEQS, RANK, RANK)
    seq_grads = jnp.stack([gram_sum(gate_proj, model_proj), gram_sum(up_proj, model_proj), gram_sum(out_proj, hidden_proj)], axis=2)
    seq_grads = seq_grads.reshape(SEQS, 3 * RANK * RANK).astype(jnp.bfloat16)
    full = contract_rows(seq_grads, queries)
    full = full / jnp.sqrt(lengths.astype(jnp.float32))[:, None]
    blocks = full.reshape(SEQS, QB, QBS)
    chosen = jnp.take_along_axis(blocks, cand[:, :, None], axis=1)
    in_use = jnp.arange(CAND, dtype=jnp.int32)[None, :] < cand_count[:, None]
    return jnp.where(in_use[:, :, None], chosen, jnp.float32(0.0))
```

```python
import jax
import jax.numpy as jnp
from jax import lax
from jax.sharding import PartitionSpec as P

QBS = 32
CAND = 8


def contract_rows(left, right):
    return lax.dot_general(
        left, right, (((1,), (1,)), ((), ())), preferred_element_type=jnp.float32
    )


def local(
    x_in,
    gate_pre,
    up_pre,
    grad_hidden,
    grad_out,
    proj_model,
    proj_hidden,
    lengths,
    queries,
    cand,
    cand_count,
):
    model_rows, hidden_rows = (
        lax.all_gather(proj_model, "dp", axis=0, tiled=True),
        lax.all_gather(proj_hidden, "dp", axis=0, tiled=True),
    )
    gate_f = gate_pre.astype(jnp.float32)
    up_f = up_pre.astype(jnp.float32)
    grad_f = grad_hidden.astype(jnp.float32)
    sig_gate = jax.nn.sigmoid(gate_f)
    hidden_act = (gate_f * sig_gate * up_f).astype(jnp.bfloat16)
    grad_gate = (grad_f * up_f * sig_gate * (1.0 + gate_f * (1.0 - sig_gate))).astype(jnp.bfloat16)
    grad_up = (grad_f * gate_f * sig_gate).astype(jnp.bfloat16)
    partial_proj = jnp.concatenate(
        [
            contract_rows(x_in, model_rows),
            contract_rows(hidden_act, hidden_rows),
            contract_rows(grad_gate, hidden_rows),
            contract_rows(grad_up, hidden_rows),
            contract_rows(grad_out, model_rows),
        ],
        axis=1,
    )
    summed = lax.psum(partial_proj, "tensor")
    rank_size = model_rows.shape[0]
    half_rank = rank_size // lax.axis_size("tensor")
    core_index = lax.axis_index("tensor")
    model_proj = summed[:, 0:rank_size]
    hidden_proj = summed[:, rank_size : 2 * rank_size]
    gate_proj = summed[:, 2 * rank_size : 3 * rank_size]
    up_proj = summed[:, 3 * rank_size : 4 * rank_size]
    out_proj = summed[:, 4 * rank_size : 5 * rank_size]
    seq_count = lengths.shape[0]
    tok_count = x_in.shape[0]
    position = lax.axis_index("dp") * tok_count + jnp.arange(tok_count, dtype=jnp.int32)
    order = jnp.arange(seq_count, dtype=jnp.int32)
    seq_ends = jnp.sum(jnp.where(order[None, :] <= order[:, None], lengths[None, :], 0), axis=1)
    seq_of = jnp.sum((seq_ends[None, :] <= position[:, None]).astype(jnp.int32), axis=1)
    onehot = (seq_of[:, None] == jnp.arange(seq_count, dtype=jnp.int32)[None, :]).astype(
        jnp.float32
    )

    def gram_sum(out_vecs, in_vecs):
        own_rows = lax.dynamic_slice_in_dim(out_vecs, core_index * half_rank, half_rank, 1)
        left = (onehot[:, :, None] * own_rows[:, None, :]).reshape(tok_count, seq_count * half_rank)
        return jnp.dot(left.T, in_vecs, precision=lax.Precision.HIGHEST).reshape(
            seq_count, half_rank, rank_size
        )

    partial_grads = jnp.stack(
        [
            gram_sum(gate_proj, model_proj),
            gram_sum(up_proj, model_proj),
            gram_sum(out_proj, hidden_proj),
        ],
        axis=2,
    )
    partial_grads = partial_grads.reshape(seq_count, half_rank * 3 * rank_size)
    slice_sums = lax.psum_scatter(partial_grads, "dp", scatter_dimension=1, tiled=True)
    slice_grads = slice_sums.astype(jnp.bfloat16)
    scale_rows = 1.0 / jnp.sqrt(lengths.astype(jnp.float32))[:, None]
    query_slice = lax.all_to_all(queries, "dp", split_axis=1, concat_axis=0, tiled=True)
    score_part = contract_rows(slice_grads, query_slice)
    full = lax.psum(score_part, ("dp", "tensor")) * scale_rows
    blocks = full.reshape(seq_count, -1, QBS)
    block_number = blocks.shape[1]
    picker = (cand[:, :, None] == jnp.arange(block_number, dtype=jnp.int32)[None, None, :]).astype(
        jnp.float32
    )
    chosen = jnp.einsum("scb,sbk->sck", picker, blocks, precision=lax.Precision.HIGHEST)
    in_use = jnp.arange(CAND, dtype=jnp.int32)[None, :] < cand_count[:, None]
    return jnp.where(in_use[:, :, None], chosen, jnp.float32(0.0))


def solution(mesh):
    placed = (
        P(("groups", "dp"), "tensor"),
        P(("groups", "dp"), "tensor"),
        P(("groups", "dp"), "tensor"),
        P(("groups", "dp"), "tensor"),
        P(("groups", "dp"), "tensor"),
        P("dp", "tensor"),
        P("dp", "tensor"),
        P("groups"),
        P(("groups", "dp"), "tensor"),
        P("groups", None),
        P("groups"),
    )
    return jax.shard_map(
        local, mesh=mesh, in_specs=placed, out_specs=P("groups", None, None), check_vma=False
    )
```

```python
import functools
import jax
import jax.numpy as jnp
from jax import lax
from jax.experimental import pallas as pl
from jax.experimental.pallas import tpu as pltpu
from jax.sharding import PartitionSpec as P

MESH = pl.DeviceIdType.MESH
F32 = jnp.float32
BF16 = jnp.bfloat16
LANES = 128
FOLDED = 16
CHUNKS = 3
SHARE = 0.36


def iota(shape, dim):
    return lax.broadcasted_iota(jnp.int32, shape, dim)


def dot_nt(left, right):
    return lax.dot_general(left, right, (((1,), (1,)), ((), ())), preferred_element_type=F32)


def dot_nn(left, right):
    return lax.dot_general(left, right, (((1,), (0,)), ((), ())), preferred_element_type=F32)


def halves(value):
    high = value.astype(BF16)
    return high, (value - high.astype(F32)).astype(BF16)


def kernel(
    dims,
    len_ref, cand_ref, count_ref,
    x_hbm, gate_hbm, up_hbm, grad_hbm, out_hbm, pm_hbm, ph_hbm, q_hbm,
    o_ref,
    gate, up, grad, act, xo, pm, ph, q, qr, w, acc_h, acc_m,
    proj, proj_other, parts, parts_in, sg, flat, finals,
    sem_in, sem_small, s_right, s_left, s_y, s_x, r_zy, r_x,
    s_pair, r_pair, s_rs, r_rs, s_ag, r_ag, s_fin, r_fin,
):
    groups, dp, tp, rows, seqs, cands = dims
    toks, ffl = gate.shape
    ml = pm.shape[1]
    fold = FOLDED // rows
    rank = rows * dp
    mfold, hfold = ml // fold, ffl // fold
    width = mfold + hfold
    chunk = width // CHUNKS
    blocks = chunk // LANES
    part = LANES * max(1, round(blocks * SHARE))
    zs = dp // 2
    half = rank // tp
    il = half // dp
    n_in = sem_in.shape[1]
    in_cols = ffl // n_in

    g = lax.axis_index("groups")
    me = lax.axis_index("dp")
    core = lax.axis_index("tensor")
    z, y = me // 2, lax.rem(me, 2)
    xx = lax.rem(g, 2)
    other_g = g + 1 - 2 * xx
    other_core = lax.rem(core + 1, tp)

    small = [
        pltpu.make_async_copy(pm_hbm, pm, sem_small.at[0]),
        pltpu.make_async_copy(ph_hbm, ph, sem_small.at[1]),
        pltpu.make_async_copy(x_hbm, xo.at[pl.ds(0, toks)], sem_small.at[2]),
        pltpu.make_async_copy(out_hbm, xo.at[pl.ds(toks, toks)], sem_small.at[3]),
        pltpu.make_async_copy(q_hbm, q, sem_small.at[4]),
    ]
    small[0].start()
    small[1].start()

    barrier = pltpu.get_barrier_semaphore()
    for step in range(1, dp * tp):
        flat_id = lax.rem(me * tp + core + step, dp * tp)
        pl.semaphore_signal(
            barrier, inc=1, device_id={"dp": flat_id // tp, "tensor": lax.rem(flat_id, tp)}, device_id_type=MESH
        )
    pl.semaphore_signal(barrier, inc=1, device_id={"groups": other_g}, device_id_type=MESH)

    def big(n, which):
        src, dst = ((gate_hbm, gate), (up_hbm, up), (grad_hbm, grad))[which]
        cols = pl.ds(n * in_cols, in_cols)
        return pltpu.make_async_copy(src.at[:, cols], dst.at[:, cols], sem_in.at[which, n])

    for n in range(n_in):
        for which in range(3):
            big(n, which).start()
    for c in small[2:]:
        c.start()

    small[0].wait()
    small[1].wait()
    mine = w.at[me]
    for src, cols, base in ((pm, mfold, 0), (ph, hfold, mfold)):
        mine[:, base : base + cols] = jnp.concatenate(
            [src[:, f * cols : (f + 1) * cols].astype(F32) for f in range(fold)], axis=0
        ).astype(BF16)
    pl.semaphore_wait(barrier, dp * tp)

    zy_cols = [pl.ds(pl.multiple_of(c * chunk + xx * part, LANES), chunk - part) for c in range(CHUNKS)]
    x_cols = [pl.ds(pl.multiple_of(c * chunk + xx * (chunk - part), LANES), part) for c in range(CHUNKS)]
    x_in_cols = [pl.ds(pl.multiple_of(c * chunk + (1 - xx) * (chunk - part), LANES), part) for c in range(CHUNKS)]

    def zy_copy(c, slot, send_sem, target):
        ref = w.at[slot, :, zy_cols[c]]
        return pltpu.make_async_remote_copy(ref, ref, send_sem, r_zy.at[c, slot], device_id=target, device_id_type=MESH)

    def x_copy(c, slot, send_sem, cols):
        ref = w.at[slot, :, cols[c]]
        return pltpu.make_async_remote_copy(
            ref, ref, send_sem, r_x.at[c, slot], device_id={"groups": other_g}, device_id_type=MESH
        )

    def slot_of(pos, col):
        return jnp.clip(pos, 0, zs - 1) * 2 + col

    def right_send(c, k):
        return zy_copy(c, slot_of(z - k, y), s_right.at[c, k], {"dp": me + 2})

    def left_send(c, k):
        return zy_copy(c, slot_of(z + k, y), s_left.at[c, k], {"dp": me - 2})

    def y_send(c, k, way):
        return zy_copy(c, slot_of(z + way * k, y), s_y.at[c, zs + way * k], {"dp": z * 2 + 1 - y})

    def x_send(c, k, way, col):
        return x_copy(c, slot_of(z + way * k, jnp.where(col == 0, y, 1 - y)), s_x.at[c, col, zs + way * k], x_cols)

    def own_step(c):
        @pl.when(z + 1 < zs)
        def _():
            right_send(c, 0).start()

        @pl.when(z >= 1)
        def _():
            left_send(c, 0).start()

        y_send(c, 0, 1).start()

    def z_step(c, k):
        @pl.when(z - k >= 0)
        def _():
            right_send(c, k).wait_recv()

            @pl.when(z + 1 < zs)
            def _():
                right_send(c, k).start()

            y_send(c, k, -1).start()
            x_send(c, k, -1, 0).start()

        @pl.when(z + k < zs)
        def _():
            left_send(c, k).wait_recv()

            @pl.when(z >= 1)
            def _():
                left_send(c, k).start()

            y_send(c, k, 1).start()
            x_send(c, k, 1, 0).start()

    def y_step(c, k):
        for way in (-1, 1) if k else (1,):

            @pl.when((z + way * k >= 0) & (z + way * k < zs))
            def _():
                slot = slot_of(z + way * k, 1 - y)
                zy_copy(c, slot, s_y.at[c, zs], {"dp": me}).wait_recv()
                x_send(c, k, way, 1).start()

    def x_wait(c):
        for step in range(1, dp):
            x_copy(c, lax.rem(me + step, dp), s_x.at[c, 0, zs], x_in_cols).wait_recv()

    for c in range(CHUNKS):
        own_step(c)

    step_cols = 4 * LANES
    while in_cols % step_cols:
        step_cols //= 2
    acts = ffl // step_cols

    def activate(base):
        for r in range(0, toks, FOLDED):
            at = (pl.ds(r, FOLDED), pl.ds(base, step_cols))
            gv, uv, dv = gate[at].astype(F32), up[at].astype(F32), grad[at].astype(F32)
            sig = 0.5 * jnp.tanh(0.5 * gv) + 0.5
            silu = gv * sig
            act[pl.ds(r, FOLDED), pl.ds(base, step_cols)] = (silu * uv).astype(BF16)
            act[pl.ds(toks + r, FOLDED), pl.ds(base, step_cols)] = (
                dv * uv * (sig * (1.0 + gv * (1.0 - sig)))
            ).astype(BF16)
            act[pl.ds(2 * toks + r, FOLDED), pl.ds(base, step_cols)] = (dv * silu).astype(BF16)

    def activate_input(n):
        for which in range(3):
            big(n, which).wait()

        @pl.loop(0, in_cols // step_cols)
        def _(i):
            activate(pl.multiple_of(n * in_cols + i * step_cols, LANES))

    def spread_queries():
        small[4].wait()
        qs = q.shape[0]
        wide = q.shape[1] // half
        for i in range(half):
            qr[i * qs : (i + 1) * qs, :] = q[:, i * wide : (i + 1) * wide]

    events = []
    for k in range(zs):
        if k:
            events += [functools.partial(z_step, c, k) for c in range(CHUNKS)]
            events += [functools.partial(y_step, c, k - 1) for c in range(CHUNKS)]
    last = [functools.partial(y_step, c, zs - 1) for c in range(CHUNKS)]

    work = [functools.partial(activate_input, n) for n in range(n_in)] + [spread_queries]
    done = 0
    for n, job in enumerate(work):
        job()
        upto = (n + 1) * len(events) // len(work)
        for e in events[done:upto]:
            e()
        done = upto

    acc_h[...] = jnp.zeros_like(acc_h)
    acc_m[...] = jnp.zeros_like(acc_m)
    lanes_w = dp * FOLDED
    small[2].wait()
    small[3].wait()

    def multiply(acc, src, total, lo, hi, base):
        if hi <= lo:
            return
        kc = 4 * LANES
        while (hi - lo) % kc:
            kc //= 2

        @pl.loop(0, (hi - lo) // kc)
        def _(i):
            at = lo + i * kc
            wv = w[:, :, pl.ds(pl.multiple_of(base + at, LANES), kc)].reshape(lanes_w, kc)
            for f in range(fold):
                sv = src[:, pl.ds(pl.multiple_of(f * total + at, LANES), kc)]
                acc[f] += dot_nt(sv, wv)

    def multiply_chunk(c):
        x_wait(c)
        lo, hi = c * chunk, (c + 1) * chunk
        multiply(acc_m, xo, mfold, lo, min(hi, mfold), 0)
        multiply(acc_h, act, hfold, max(lo - mfold, 0), hi - mfold, mfold)

    last[0]()
    for c in range(CHUNKS):
        if c + 1 < CHUNKS:
            last[c + 1]()
        multiply_chunk(c)

    lane, col = iota((lanes_w, rank), 0), iota((lanes_w, rank), 1)
    for acc, base in ((acc_h, 0), (acc_m, 3 * toks)):
        total = None
        for f in range(fold):
            local = lax.rem(lane, FOLDED) - f * rows
            pick = ((lane // FOLDED) * rows + local == col) & (local >= 0) & (local < rows)
            pick = pick.astype(F32).astype(BF16)
            high, low = halves(acc[f])
            term = dot_nn(high, pick) + dot_nn(low, pick)
            total = term if total is None else total + term
        proj[pl.ds(base, acc.shape[1]), :] = total
    pair = pltpu.make_async_remote_copy(
        proj, proj_other, s_pair, r_pair, device_id={"tensor": other_core}, device_id_type=MESH
    )
    pair.start()

    n_rows = seqs * half
    slice_rows = seqs * il
    rr = iota((n_rows, toks), 0)
    seq_of_row = lax.rem(rr, slice_rows) // il
    position = me * toks + iota((n_rows, toks), 1)
    start = jnp.int32(0)
    inside = jnp.zeros((n_rows, toks), jnp.bool_)
    for s in range(seqs):
        stop = start + len_ref[s]
        inside = inside | ((seq_of_row == s) & (position >= start) & (position < stop))
        start = stop
    r2, c2 = iota((n_rows, rank), 0), iota((n_rows, rank), 1)
    chosen_rank = core * half + (r2 // slice_rows) * il + lax.rem(r2, il)
    pick_left = (c2 == chosen_rank).astype(F32).astype(BF16)
    pair.wait()

    def vectors(m):
        at = pl.ds(m * toks, toks)
        return proj[at, :] + proj_other[at, :]

    hidden_v, gate_v, up_v, model_v, out_v = [vectors(m) for m in range(5)]
    for m, (a, b) in enumerate(((gate_v, model_v), (up_v, model_v), (out_v, hidden_v))):
        high, low = halves(a)
        left = jnp.where(inside, dot_nt(pick_left, high) + dot_nt(pick_left, low), 0.0)
        lh, ll = halves(left)
        bh, bl = halves(b)
        gram = dot_nn(lh, bh) + (dot_nn(lh, bl) + dot_nn(ll, bh))
        for d in range(dp):
            parts[d, :, m * rank : (m + 1) * rank] = gram[d * slice_rows : (d + 1) * slice_rows]

    def rs(step):
        to = lax.rem(me + step, dp)
        return pltpu.make_async_remote_copy(
            parts.at[to], parts_in.at[step], s_rs.at[step], r_rs.at[step], device_id={"dp": to}, device_id_type=MESH
        )

    def ag(step):
        return pltpu.make_async_remote_copy(
            sg.at[0], sg.at[step], s_ag.at[step], r_ag.at[step],
            device_id={"dp": lax.rem(me + step, dp)}, device_id_type=MESH,
        )

    for step in range(1, dp):
        rs(step).start()
    total = parts[me]
    for step in range(1, dp):
        rs(step).wait_recv()
        total = total + parts_in[step]
    sg[0] = total.astype(BF16).astype(F32)
    for step in range(1, dp):
        ag(step).start()
    flat[0:slice_rows, :] = sg[0]
    for step in range(1, dp):
        ag(step).wait_recv()
        flat[step * slice_rows : (step + 1) * slice_rows, :] = sg[step]

    qs = q.shape[0]
    big_scores = dot_nt(flat[...].astype(BF16), qr[...])
    br, bc = iota(big_scores.shape, 0), iota(big_scores.shape, 1)
    from_dev = lax.rem(me + dp - br // slice_rows, dp)
    same = (from_dev * il + lax.rem(br, il)) == bc // qs
    high, low = halves(jnp.where(same, big_scores, 0.0))
    sr, sc = iota((8, n_rows), 0), iota((8, n_rows), 1)
    sum_rows = (lax.rem(sc, slice_rows) // il == sr).astype(F32).astype(BF16)
    by_seq = dot_nn(sum_rows, high) + dot_nn(sum_rows, low)
    fr, fc = iota((half * qs, LANES), 0), iota((half * qs, LANES), 1)
    fold_q = (lax.rem(fr, qs) == fc).astype(F32).astype(BF16)
    high, low = halves(by_seq)
    finals[me * tp + core] = dot_nn(high, fold_q) + dot_nn(low, fold_q)

    def fin(step):
        mine = me * tp + core
        to = lax.rem(mine + step, dp * tp)
        return pltpu.make_async_remote_copy(
            finals.at[mine], finals.at[mine], s_fin.at[step], r_fin.at[step],
            device_id={"dp": to // tp, "tensor": lax.rem(to, tp)}, device_id_type=MESH,
        )

    for step in range(1, dp * tp):
        fin(step).start()

    row = iota((8, LANES), 0)
    lens = jnp.ones((8, LANES), F32)
    for s in range(seqs):
        lens = jnp.where(row == s, len_ref[s].astype(F32), lens)
    scale = 1.0 / jnp.sqrt(lens)
    wanted = []
    for c in range(cands):
        v = jnp.full((8, LANES), -1, jnp.int32)
        for s in range(seqs):
            v = jnp.where(row == s, jnp.where(c < count_ref[s], cand_ref[s, c], -1), v)
        wanted.append(v)
    for step in range(1, dp * tp):
        fin(step).wait_recv()
    found = [jnp.zeros((8, LANES), F32) for _ in range(cands)]
    for b in range(dp):
        block = finals[b * tp]
        for t in range(1, tp):
            block = block + finals[b * tp + t]
        block = block * scale
        for c in range(cands):
            found[c] = jnp.where(wanted[c] == b, block, found[c])
    for c in range(cands):
        o_ref[:, c, :] = found[c][:seqs, :qs]

    for step in range(1, dp * tp):
        fin(step).wait_send()
    for step in range(1, dp):
        rs(step).wait_send()
        ag(step).wait_send()
    for c in range(CHUNKS):
        for k in range(zs):

            @pl.when((z - k >= 0) & (z + 1 < zs))
            def _():
                right_send(c, k).wait_send()

            @pl.when((z + k < zs) & (z >= 1))
            def _():
                left_send(c, k).wait_send()

            for way in (-1, 1) if k else (1,):

                @pl.when((z + way * k >= 0) & (z + way * k < zs))
                def _():
                    y_send(c, k, way).wait_send()
                    x_send(c, k, way, 1).wait_send()
                    if k:
                        x_send(c, k, way, 0).wait_send()


def local(groups, dp, tp, x_in, gate_pre, up_pre, grad_hidden, grad_out, proj_model, proj_hidden, lengths, queries, cand, cand_count):
    toks, ffl = gate_pre.shape
    rows, ml = proj_model.shape
    seqs, cands = cand.shape
    qs, feats = queries.shape
    rank = rows * dp
    half = rank // tp
    fold = FOLDED // rows
    width = (ml + ffl) // fold
    zs = dp // 2
    slice_rows = seqs * (half // dp)
    n_in = 7
    dma = pltpu.SemaphoreType.DMA
    any_spec = pl.BlockSpec(memory_space=pl.ANY)
    smem = pl.BlockSpec(memory_space=pltpu.SMEM)
    return pl.pallas_call(
        functools.partial(kernel, (groups, dp, tp, rows, seqs, cands)),
        out_shape=jax.ShapeDtypeStruct((seqs, cands, qs), F32),
        in_specs=[smem] * 3 + [any_spec] * 8,
        out_specs=pl.BlockSpec(memory_space=pltpu.VMEM),
        scratch_shapes=[
            pltpu.VMEM((toks, ffl), BF16),
            pltpu.VMEM((toks, ffl), BF16),
            pltpu.VMEM((toks, ffl), BF16),
            pltpu.VMEM((3 * toks, ffl), BF16),
            pltpu.VMEM((2 * toks, ml), BF16),
            pltpu.VMEM((rows, ml), BF16),
            pltpu.VMEM((rows, ffl), BF16),
            pltpu.VMEM((qs, feats), BF16),
            pltpu.VMEM((half * qs, feats // half), BF16),
            pltpu.VMEM((dp, FOLDED, width), BF16),
            pltpu.VMEM((fold, 3 * toks, dp * FOLDED), F32),
            pltpu.VMEM((fold, 2 * toks, dp * FOLDED), F32),
            pltpu.VMEM((5 * toks, rank), F32),
            pltpu.VMEM((5 * toks, rank), F32),
            pltpu.VMEM((dp, slice_rows, 3 * rank), F32),
            pltpu.VMEM((dp, slice_rows, 3 * rank), F32),
            pltpu.VMEM((dp, slice_rows, 3 * rank), F32),
            pltpu.VMEM((seqs * half, 3 * rank), F32),
            pltpu.VMEM((dp * tp, 8, LANES), F32),
            dma((3, n_in)),
            dma((5,)),
            dma((CHUNKS, zs)),
            dma((CHUNKS, zs)),
            dma((CHUNKS, 2 * zs)),
            dma((CHUNKS, 2, 2 * zs)),
            dma((CHUNKS, dp)),
            dma((CHUNKS, dp)),
            dma,
            dma,
            dma((dp,)),
            dma((dp,)),
            dma((dp,)),
            dma((dp,)),
            dma((dp * tp,)),
            dma((dp * tp,)),
        ],
        compiler_params=pltpu.CompilerParams(
            collective_id=0, has_side_effects=True, vmem_limit_bytes=56 * 1024 * 1024
        ),
    )(lengths, cand, cand_count, x_in, gate_pre, up_pre, grad_hidden, grad_out, proj_model, proj_hidden, queries)


def solution(mesh):
    placed = (
        P(("groups", "dp"), "tensor"),
        P(("groups", "dp"), "tensor"),
        P(("groups", "dp"), "tensor"),
        P(("groups", "dp"), "tensor"),
        P(("groups", "dp"), "tensor"),
        P("dp", "tensor"),
        P("dp", "tensor"),
        P("groups"),
        P(("groups", "dp"), "tensor"),
        P("groups", None),
        P("groups"),
    )
    sizes = mesh.shape
    return jax.shard_map(
        functools.partial(local, sizes["groups"], sizes["dp"], sizes["tensor"]),
        mesh=mesh, in_specs=placed, out_specs=P("groups", None, None), check_vma=False,
    )
```

```python
import functools
import jax
import jax.numpy as jnp
from jax import lax
from jax.experimental import pallas as pl
from jax.experimental.pallas import tpu as pltpu
from jax.sharding import PartitionSpec as P

MESH = pl.DeviceIdType.MESH
F32 = jnp.float32
BF16 = jnp.bfloat16
LANES = 128
FOLDED = 16
CHUNKS = 2
SHARE = 0.3


def iota(shape, dim):
    return lax.broadcasted_iota(jnp.int32, shape, dim)


def dot_nt(left, right):
    return lax.dot_general(left, right, (((1,), (1,)), ((), ())), preferred_element_type=F32)


def dot_nn(left, right):
    return lax.dot_general(left, right, (((1,), (0,)), ((), ())), preferred_element_type=F32)


def halves(value):
    high = value.astype(BF16)
    return high, (value - high.astype(F32)).astype(BF16)


def kernel(
    dims,
    len_ref, cand_ref, count_ref,
    x_hbm, gate_hbm, up_hbm, grad_hbm, out_hbm, pm_hbm, ph_hbm, q_hbm,
    o_ref,
    gate, up, grad, act, xo, pm, ph, q, qr, w, acc_h, acc_m,
    proj, proj_other, parts, parts_in, sg, flat, halved, finals,
    sem_in, sem_small, s_right, s_left, s_y, s_x, r_zy, r_x,
    s_pair, r_pair, s_rs, r_rs, s_ag, r_ag, s_fin, r_fin,
):
    groups, dp, tp, rows, seqs, cands = dims
    toks, ffl = gate.shape
    ml = pm.shape[1]
    fold = FOLDED // rows
    rank = rows * dp
    mfold, hfold = ml // fold, ffl // fold
    width = mfold + hfold
    chunk = width // CHUNKS
    blocks = chunk // LANES
    part = LANES * max(1, round(blocks * SHARE))
    zs = dp // 2
    half = rank // tp
    il = half // dp
    n_in = sem_in.shape[1]
    in_cols = ffl // n_in

    g = lax.axis_index("groups")
    me = lax.axis_index("dp")
    core = lax.axis_index("tensor")
    z, y = me // 2, lax.rem(me, 2)
    xx = lax.rem(g, 2)
    other_g = g + 1 - 2 * xx
    other_core = lax.rem(core + 1, tp)

    small = [
        pltpu.make_async_copy(pm_hbm, pm, sem_small.at[0]),
        pltpu.make_async_copy(ph_hbm, ph, sem_small.at[1]),
        pltpu.make_async_copy(x_hbm, xo.at[pl.ds(0, toks)], sem_small.at[2]),
        pltpu.make_async_copy(out_hbm, xo.at[pl.ds(toks, toks)], sem_small.at[3]),
        pltpu.make_async_copy(q_hbm, q, sem_small.at[4]),
    ]
    small[0].start()
    small[1].start()

    barrier = pltpu.get_barrier_semaphore()
    for target in ({"dp": z * 2 + 1 - y}, {"groups": other_g}, {"tensor": other_core}):
        pl.semaphore_signal(barrier, inc=1, device_id=target, device_id_type=MESH)

    @pl.when(z + 1 < zs)
    def _():
        pl.semaphore_signal(barrier, inc=1, device_id={"dp": me + 2}, device_id_type=MESH)

    @pl.when(z >= 1)
    def _():
        pl.semaphore_signal(barrier, inc=1, device_id={"dp": me - 2}, device_id_type=MESH)

    def big(n, which):
        src, dst = ((gate_hbm, gate), (up_hbm, up), (grad_hbm, grad))[which]
        cols = pl.ds(n * in_cols, in_cols)
        return pltpu.make_async_copy(src.at[:, cols], dst.at[:, cols], sem_in.at[which, n])

    for n in range(n_in):
        for which in range(3):
            big(n, which).start()
    for c in small[2:]:
        c.start()

    small[0].wait()
    small[1].wait()
    mine = w.at[me]
    for src, cols, base in ((pm, mfold, 0), (ph, hfold, mfold)):
        mine[:, base : base + cols] = jnp.concatenate(
            [src[:, f * cols : (f + 1) * cols].astype(F32) for f in range(fold)], axis=0
        ).astype(BF16)
    pl.semaphore_wait(barrier, 3 + (z + 1 < zs).astype(jnp.int32) + (z >= 1).astype(jnp.int32))

    zy_cols = [pl.ds(pl.multiple_of(c * chunk + xx * part, LANES), chunk - part) for c in range(CHUNKS)]
    x_cols = [pl.ds(pl.multiple_of(c * chunk + xx * (chunk - part), LANES), part) for c in range(CHUNKS)]
    x_in_cols = [pl.ds(pl.multiple_of(c * chunk + (1 - xx) * (chunk - part), LANES), part) for c in range(CHUNKS)]

    def zy_copy(c, slot, send_sem, target):
        ref = w.at[slot, :, zy_cols[c]]
        return pltpu.make_async_remote_copy(ref, ref, send_sem, r_zy.at[c, slot], device_id=target, device_id_type=MESH)

    def x_copy(c, slot, send_sem, cols):
        ref = w.at[slot, :, cols[c]]
        return pltpu.make_async_remote_copy(
            ref, ref, send_sem, r_x.at[c, slot], device_id={"groups": other_g}, device_id_type=MESH
        )

    def slot_of(pos, col):
        return jnp.clip(pos, 0, zs - 1) * 2 + col

    def right_send(c, k):
        return zy_copy(c, slot_of(z - k, y), s_right.at[c, k], {"dp": me + 2})

    def left_send(c, k):
        return zy_copy(c, slot_of(z + k, y), s_left.at[c, k], {"dp": me - 2})

    def y_send(c, k, way):
        return zy_copy(c, slot_of(z + way * k, y), s_y.at[c, zs + way * k], {"dp": z * 2 + 1 - y})

    def x_send(c, k, way, col):
        return x_copy(c, slot_of(z + way * k, jnp.where(col == 0, y, 1 - y)), s_x.at[c, col, zs + way * k], x_cols)

    def own_step(c):
        @pl.when(z + 1 < zs)
        def _():
            right_send(c, 0).start()

        @pl.when(z >= 1)
        def _():
            left_send(c, 0).start()

        y_send(c, 0, 1).start()

    def z_step(c, k):
        @pl.when(z - k >= 0)
        def _():
            right_send(c, k).wait_recv()

            @pl.when(z + 1 < zs)
            def _():
                right_send(c, k).start()

            y_send(c, k, -1).start()
            x_send(c, k, -1, 0).start()

        @pl.when(z + k < zs)
        def _():
            left_send(c, k).wait_recv()

            @pl.when(z >= 1)
            def _():
                left_send(c, k).start()

            y_send(c, k, 1).start()
            x_send(c, k, 1, 0).start()

    def y_step(c, k):
        for way in (-1, 1) if k else (1,):

            @pl.when((z + way * k >= 0) & (z + way * k < zs))
            def _():
                slot = slot_of(z + way * k, 1 - y)
                zy_copy(c, slot, s_y.at[c, zs], {"dp": me}).wait_recv()
                x_send(c, k, way, 1).start()

    def x_wait(c):
        for step in range(1, dp):
            x_copy(c, lax.rem(me + step, dp), s_x.at[c, 0, zs], x_in_cols).wait_recv()

    for c in range(CHUNKS):
        own_step(c)

    step_cols = 4 * LANES
    while in_cols % step_cols:
        step_cols //= 2
    acts = ffl // step_cols

    def activate(base):
        for r in range(0, toks, FOLDED):
            at = (pl.ds(r, FOLDED), pl.ds(base, step_cols))
            gv, uv, dv = gate[at].astype(F32), up[at].astype(F32), grad[at].astype(F32)
            sig = 0.5 * jnp.tanh(0.5 * gv) + 0.5
            silu = gv * sig
            act[pl.ds(r, FOLDED), pl.ds(base, step_cols)] = (silu * uv).astype(BF16)
            act[pl.ds(toks + r, FOLDED), pl.ds(base, step_cols)] = (
                dv * uv * (sig * (1.0 + gv * (1.0 - sig)))
            ).astype(BF16)
            act[pl.ds(2 * toks + r, FOLDED), pl.ds(base, step_cols)] = (dv * silu).astype(BF16)

    def activate_input(n):
        for which in range(3):
            big(n, which).wait()

        @pl.loop(0, in_cols // step_cols)
        def _(i):
            activate(pl.multiple_of(n * in_cols + i * step_cols, LANES))

    def spread_queries():
        small[4].wait()
        qs = q.shape[0]
        wide = q.shape[1] // half
        for i in range(half):
            qr[i * qs : (i + 1) * qs, :] = q[:, i * wide : (i + 1) * wide]

    events = []
    for k in range(zs):
        if k:
            events += [functools.partial(z_step, c, k) for c in range(CHUNKS)]
            events += [functools.partial(y_step, c, k - 1) for c in range(CHUNKS)]
    last = [functools.partial(y_step, c, zs - 1) for c in range(CHUNKS)]

    work = [functools.partial(activate_input, n) for n in range(n_in)] + [spread_queries]
    done = 0
    for n, job in enumerate(work):
        job()
        upto = (n + 1) * len(events) // len(work)
        for e in events[done:upto]:
            e()
        done = upto

    acc_h[...] = jnp.zeros_like(acc_h)
    acc_m[...] = jnp.zeros_like(acc_m)
    lanes_w = dp * FOLDED
    small[2].wait()
    small[3].wait()

    def multiply(acc, src, total, lo, hi, base):
        if hi <= lo:
            return
        units = (hi - lo) // LANES
        kc = LANES * max(n for n in range(1, 13) if units % n == 0)

        @pl.loop(0, (hi - lo) // kc)
        def _(i):
            at = lo + i * kc
            wv = w[:, :, pl.ds(pl.multiple_of(base + at, LANES), kc)].reshape(lanes_w, kc)
            for f in range(fold):
                sv = src[:, pl.ds(pl.multiple_of(f * total + at, LANES), kc)]
                acc[f] += dot_nt(sv, wv)

    def multiply_chunk(c):
        x_wait(c)
        lo, hi = c * chunk, (c + 1) * chunk
        multiply(acc_m, xo, mfold, lo, min(hi, mfold), 0)
        multiply(acc_h, act, hfold, max(lo - mfold, 0), hi - mfold, mfold)

    last[0]()
    for c in range(CHUNKS):
        if c + 1 < CHUNKS:
            last[c + 1]()
        multiply_chunk(c)

    lane, col = iota((lanes_w, rank), 0), iota((lanes_w, rank), 1)
    for acc, base in ((acc_h, 0), (acc_m, 3 * toks)):
        total = None
        for f in range(fold):
            local = lax.rem(lane, FOLDED) - f * rows
            pick = ((lane // FOLDED) * rows + local == col) & (local >= 0) & (local < rows)
            pick = pick.astype(F32).astype(BF16)
            high, low = halves(acc[f])
            term = dot_nn(high, pick) + dot_nn(low, pick)
            total = term if total is None else total + term
        proj[pl.ds(base, acc.shape[1]), :] = total
    pair = pltpu.make_async_remote_copy(
        proj, proj_other, s_pair.at[0], r_pair.at[0], device_id={"tensor": other_core}, device_id_type=MESH
    )
    pair.start()

    n_rows = seqs * half
    slice_rows = seqs * il
    rr = iota((n_rows, toks), 0)
    seq_of_row = lax.rem(rr, slice_rows) // il
    position = me * toks + iota((n_rows, toks), 1)
    start = jnp.int32(0)
    inside = jnp.zeros((n_rows, toks), jnp.bool_)
    for s in range(seqs):
        stop = start + len_ref[s]
        inside = inside | ((seq_of_row == s) & (position >= start) & (position < stop))
        start = stop
    r2, c2 = iota((n_rows, rank), 0), iota((n_rows, rank), 1)
    chosen_rank = core * half + (r2 // slice_rows) * il + lax.rem(r2, il)
    pick_left = (c2 == chosen_rank).astype(F32).astype(BF16)
    pair.wait()

    def vectors(m):
        at = pl.ds(m * toks, toks)
        return proj[at, :] + proj_other[at, :]

    hidden_v, gate_v, up_v, model_v, out_v = [vectors(m) for m in range(5)]
    for m, (a, b) in enumerate(((gate_v, model_v), (up_v, model_v), (out_v, hidden_v))):
        high, low = halves(a)
        left = jnp.where(inside, dot_nt(pick_left, high) + dot_nt(pick_left, low), 0.0)
        lh, ll = halves(left)
        bh, bl = halves(b)
        gram = dot_nn(lh, bh) + (dot_nn(lh, bl) + dot_nn(ll, bh))
        for d in range(dp):
            parts[d, :, m * rank : (m + 1) * rank] = gram[d * slice_rows : (d + 1) * slice_rows].astype(BF16)

    def rs(step):
        to = lax.rem(me + step, dp)
        return pltpu.make_async_remote_copy(
            parts.at[to], parts_in.at[step], s_rs.at[step], r_rs.at[step], device_id={"dp": to}, device_id_type=MESH
        )

    def ag(step):
        return pltpu.make_async_remote_copy(
            sg.at[0], sg.at[step], s_ag.at[step], r_ag.at[step],
            device_id={"dp": lax.rem(me + step, dp)}, device_id_type=MESH,
        )

    for step in range(1, dp):
        rs(step).start()
    total = parts[me].astype(F32)
    for step in range(1, dp):
        rs(step).wait_recv()
        total = total + parts_in[step].astype(F32)
    sg[0] = total.astype(BF16)
    for step in range(1, dp):
        ag(step).start()
    flat[0:slice_rows, :] = sg[0]
    for step in range(1, dp):
        ag(step).wait_recv()
        flat[step * slice_rows : (step + 1) * slice_rows, :] = sg[step]

    qs = q.shape[0]
    big_scores = dot_nt(flat[...], qr[...])
    br, bc = iota(big_scores.shape, 0), iota(big_scores.shape, 1)
    from_dev = lax.rem(me + dp - br // slice_rows, dp)
    same = (from_dev * il + lax.rem(br, il)) == bc // qs
    high, low = halves(jnp.where(same, big_scores, 0.0))
    sr, sc = iota((8, n_rows), 0), iota((8, n_rows), 1)
    sum_rows = (lax.rem(sc, slice_rows) // il == sr).astype(F32).astype(BF16)
    by_seq = dot_nn(sum_rows, high) + dot_nn(sum_rows, low)
    fr, fc = iota((half * qs, LANES), 0), iota((half * qs, LANES), 1)
    fold_q = (lax.rem(fr, qs) == fc).astype(F32).astype(BF16)
    high, low = halves(by_seq)
    halved[0] = dot_nn(high, fold_q) + dot_nn(low, fold_q)
    score_pair = pltpu.make_async_remote_copy(
        halved.at[0], halved.at[1], s_pair.at[1], r_pair.at[1], device_id={"tensor": other_core}, device_id_type=MESH
    )
    score_pair.start()

    def fin(step):
        return pltpu.make_async_remote_copy(
            finals.at[0], finals.at[step], s_fin.at[step], r_fin.at[step],
            device_id={"dp": lax.rem(me + step, dp)}, device_id_type=MESH,
        )

    row = iota((8, LANES), 0)
    lens = jnp.ones((8, LANES), F32)
    for s in range(seqs):
        lens = jnp.where(row == s, len_ref[s].astype(F32), lens)
    scale = 1.0 / jnp.sqrt(lens)
    wanted = []
    for c in range(cands):
        v = jnp.full((8, LANES), -1, jnp.int32)
        for s in range(seqs):
            v = jnp.where(row == s, jnp.where(c < count_ref[s], cand_ref[s, c], -1), v)
        wanted.append(v)
    found = [jnp.zeros((8, LANES), F32) for _ in range(cands)]
    score_pair.wait()
    finals[0] = (halved[0] + halved[1]) * scale
    for step in range(1, dp):
        fin(step).start()
    for step in range(dp):
        if step:
            fin(step).wait_recv()
        block = finals[step]
        b = lax.rem(me + dp - step, dp)
        for c in range(cands):
            found[c] = jnp.where(wanted[c] == b, block, found[c])
    for c in range(cands):
        o_ref[:, c, :] = found[c][:seqs, :qs]

    for step in range(1, dp):
        fin(step).wait_send()
        rs(step).wait_send()
        ag(step).wait_send()
    for c in range(CHUNKS):
        for k in range(zs):

            @pl.when((z - k >= 0) & (z + 1 < zs))
            def _():
                right_send(c, k).wait_send()

            @pl.when((z + k < zs) & (z >= 1))
            def _():
                left_send(c, k).wait_send()

            for way in (-1, 1) if k else (1,):

                @pl.when((z + way * k >= 0) & (z + way * k < zs))
                def _():
                    y_send(c, k, way).wait_send()
                    x_send(c, k, way, 1).wait_send()
                    if k:
                        x_send(c, k, way, 0).wait_send()


def local(groups, dp, tp, x_in, gate_pre, up_pre, grad_hidden, grad_out, proj_model, proj_hidden, lengths, queries, cand, cand_count):
    toks, ffl = gate_pre.shape
    rows, ml = proj_model.shape
    seqs, cands = cand.shape
    qs, feats = queries.shape
    rank = rows * dp
    half = rank // tp
    fold = FOLDED // rows
    width = (ml + ffl) // fold
    zs = dp // 2
    slice_rows = seqs * (half // dp)
    n_in = 7
    dma = pltpu.SemaphoreType.DMA
    any_spec = pl.BlockSpec(memory_space=pl.ANY)
    smem = pl.BlockSpec(memory_space=pltpu.SMEM)
    return pl.pallas_call(
        functools.partial(kernel, (groups, dp, tp, rows, seqs, cands)),
        out_shape=jax.ShapeDtypeStruct((seqs, cands, qs), F32),
        in_specs=[smem] * 3 + [any_spec] * 8,
        out_specs=pl.BlockSpec(memory_space=pltpu.VMEM),
        scratch_shapes=[
            pltpu.VMEM((toks, ffl), BF16),
            pltpu.VMEM((toks, ffl), BF16),
            pltpu.VMEM((toks, ffl), BF16),
            pltpu.VMEM((3 * toks, ffl), BF16),
            pltpu.VMEM((2 * toks, ml), BF16),
            pltpu.VMEM((rows, ml), BF16),
            pltpu.VMEM((rows, ffl), BF16),
            pltpu.VMEM((qs, feats), BF16),
            pltpu.VMEM((half * qs, feats // half), BF16),
            pltpu.VMEM((dp, FOLDED, width), BF16),
            pltpu.VMEM((fold, 3 * toks, dp * FOLDED), F32),
            pltpu.VMEM((fold, 2 * toks, dp * FOLDED), F32),
            pltpu.VMEM((5 * toks, rank), F32),
            pltpu.VMEM((5 * toks, rank), F32),
            pltpu.VMEM((dp, slice_rows, 3 * rank), BF16),
            pltpu.VMEM((dp, slice_rows, 3 * rank), BF16),
            pltpu.VMEM((dp, slice_rows, 3 * rank), BF16),
            pltpu.VMEM((seqs * half, 3 * rank), BF16),
            pltpu.VMEM((tp, 8, LANES), F32),
            pltpu.VMEM((dp, 8, LANES), F32),
            dma((3, n_in)),
            dma((5,)),
            dma((CHUNKS, zs)),
            dma((CHUNKS, zs)),
            dma((CHUNKS, 2 * zs)),
            dma((CHUNKS, 2, 2 * zs)),
            dma((CHUNKS, dp)),
            dma((CHUNKS, dp)),
            dma((2,)),
            dma((2,)),
            dma((dp,)),
            dma((dp,)),
            dma((dp,)),
            dma((dp,)),
            dma((dp,)),
            dma((dp,)),
        ],
        compiler_params=pltpu.CompilerParams(
            collective_id=0, has_side_effects=True, vmem_limit_bytes=56 * 1024 * 1024
        ),
    )(lengths, cand, cand_count, x_in, gate_pre, up_pre, grad_hidden, grad_out, proj_model, proj_hidden, queries)


def solution(mesh):
    placed = (
        P(("groups", "dp"), "tensor"),
        P(("groups", "dp"), "tensor"),
        P(("groups", "dp"), "tensor"),
        P(("groups", "dp"), "tensor"),
        P(("groups", "dp"), "tensor"),
        P("dp", "tensor"),
        P("dp", "tensor"),
        P("groups"),
        P(("groups", "dp"), "tensor"),
        P("groups", None),
        P("groups"),
    )
    sizes = mesh.shape
    return jax.shard_map(
        functools.partial(local, sizes["groups"], sizes["dp"], sizes["tensor"]),
        mesh=mesh, in_specs=placed, out_specs=P("groups", None, None), check_vma=False,
    )
```
